256 devices in a mesh: node: 16 (over y, z_lo), local: 16 (over z_hi, x, core).
Axes of the slice: x: 4, y: 4, z: 8 (z_hi: 2, z_lo: 4; z = z_hi * 4 + z_lo), core: 2. Of those that a mesh axis runs over, the one named last changes fastest.
Arguments:
- hidden: bfloat16 [6144, 11264], P('node', 'local'), may hold values from -6 to 6
- codes: bfloat16 [11264, 8192], P('local', 'node'), may hold values from -127 to 127, as said below
- scales: float32 [11264, 32], P('local', 'node'), may hold values from 4e-05 to 0.0004
- upstream: bfloat16 [6144, 8192], P('node', 'local'), may hold values from -6 to 6
Outputs:
- mixed: bfloat16 [6144, 8192], P('node', 'local')
- hidden_grad: bfloat16 [6144, 11264], P('node', 'local')
- weight_grad: float32 [11264, 8192], P('local', 'node')
The draws below stay inside these ranges and needn't reach their ends.
Inputs may be any that keep to these rules, and one draw needn't show every extreme that they name: codes are whole numbers.
All inputs are finite; a program needn't handle non-finite values.
Results may differ from the reference program's by a relative error of at most 0.023.
Values may be sent and summed in bfloat16 or wider, within the bound.
No kernel may reach another device: no remote copies, remote signals or barrier semaphores. Data moves between devices by JAX's collectives and lax.ppermute only.
A program may use at most 128 MiB of HBM per device.

```python
import math
import jax
import jax.numpy as jnp
from jax import lax

D = 8192
FF = 11264
BLOCK = 256
TOK_NODE = 384
TOKENS = 6144
SCALE_COLS = 32
N_NODE = 16
N_LOCAL = 16


def draw_codes(key, part):
    key = jax.random.fold_in(key, 7)
    return jax.random.randint(key, (FF, D), -127, 128).astype(jnp.float32).astype(jnp.bfloat16)


def strengthened(drawn, key, source, target, shards_of, factor):
    def block_of(dim):
        return (jnp.arange(drawn.shape[dim]) // (drawn.shape[dim] // shards_of)).reshape((-1,) + (1,) * (drawn.ndim - 1 - dim))

    one_side = jax.random.permutation(key, shards_of)[block_of(target)]
    other_side = (block_of(target) + shards_of // 2) % shards_of
    return jnp.where((block_of(source) == one_side) | (block_of(source) == other_side), factor * drawn, drawn)


def steps_of(rng, dims, shards, least, high):
    loudness, own = 1.0, jax.random.fold_in(rng, 6)
    for position, blocks in shards:
        heights = jnp.exp(jax.random.uniform(jax.random.fold_in(own, position), (blocks,), jnp.float32, least / len(shards), high / len(shards)))
        loudness = loudness * jnp.repeat(heights, dims[position] // blocks).reshape([-1 if axis == position else 1 for axis in range(len(dims))])
    return loudness


def scatter_about(key, extent, scale, most, split=(), held_as=jnp.bfloat16):
    entries = jax.random.normal(key, extent, jnp.float32) * scale
    if len(split) > 0:
        entries = steps_of(key, extent, split, -0.22, 0.18) * entries
    return jnp.clip(entries, min=-most, max=most).astype(held_as)


def gaussian_with(stream_key, dims, scale, limit, pieces, heavy, kind=jnp.bfloat16):
    entries = scale * jax.random.normal(stream_key, dims, jnp.float32)
    if pieces:
        entries = entries * steps_of(stream_key, dims, pieces, -0.22, 0.18)
    return jnp.clip(strengthened(entries, jax.random.fold_in(stream_key, 3), *heavy), -limit, limit).astype(kind)


def setup_inputs(seed: int = 0) -> dict:
    key_list = jax.random.split(jax.random.key(seed), 5)
    hidden = scatter_about(key_list[0], (TOKENS, FF), 1.0, 6.0, ((0, 16), (1, 16)))
    codes = draw_codes(jax.random.fold_in(key_list[4], 71), 0)
    scales = jnp.clip(jnp.exp(math.log(0.0004) - 2.3025851 * jax.random.uniform(key_list[2], (FF, SCALE_COLS), jnp.float32) ** steps_of(key_list[2], (FF, SCALE_COLS), ((0, 16), (1, 16)), -0.2, 0.2)), 3.9999998989515007e-05, 0.0004)
    upstream = gaussian_with(key_list[3], (TOKENS, D), 1.0, 6.0, ((0, 16), (1, 16)), (0, 1, 16, 2.0))
    return {"hidden": hidden, "codes": codes, "scales": scales, "upstream": upstream}


def reference(hidden, codes, scales, upstream):
    weight = (codes.astype(jnp.float32) * jnp.repeat(scales, BLOCK, axis=1)).astype(jnp.bfloat16)
    width = FF // N_LOCAL

    def add_group(index, total):
        rows = lax.dynamic_slice_in_dim(hidden, index * width, width, 1)
        slab = lax.dynamic_slice_in_dim(weight, index * width, width, 0)
        partial_value = jnp.dot(rows, slab, preferred_element_type=jnp.float32).astype(jnp.bfloat16)
        partial_value = lax.optimization_barrier(partial_value)
        return total + partial_value.astype(jnp.float32)
    mixed = lax.fori_loop(0, N_LOCAL, add_group, jnp.zeros((TOKENS, D), jnp.float32)).astype(jnp.bfloat16)
    hidden_grad = lax.dot_general(upstream, weight, (((1,), (1,)), ((), ())), preferred_element_type=jnp.float32).astype(jnp.bfloat16)
    factor = 1.0 / math.sqrt(TOKENS)

    def add_tokens(index, total):
        rows = lax.dynamic_slice_in_dim(hidden, index * TOK_NODE, TOK_NODE, 0)
        cots = lax.dynamic_slice_in_dim(upstream, index * TOK_NODE, TOK_NODE, 0)
        term = lax.dot_general(rows, cots, (((0,), (0,)), ((), ())), preferred_element_type=jnp.float32)
        term = (term * factor).astype(jnp.bfloat16)
        term = lax.optimization_barrier(term)
        return total + term.astype(jnp.float32)
    weight_grad = lax.fori_loop(0, N_NODE, add_tokens, jnp.zeros((FF, D), jnp.float32))
    return (mixed, hidden_grad, weight_grad)
```

```python
import functools
import math

import jax
import jax.numpy as jnp
from jax import lax
from jax.experimental import pallas as pl
from jax.experimental.pallas import tpu as pltpu
from jax.sharding import Mesh, PartitionSpec as P
import numpy as np

BLOCK = 256
AXES = ("y", "zl", "zh", "x", "c")
DIMS = (4, 4, 2, 4, 2)
VMEM_LIMIT = 50 * 1024 * 1024


def permute(array, target):
    pairs = []
    for index, source in enumerate(np.ndindex(*DIMS)):
        pairs.append((index, int(np.ravel_multi_index(target(*source), DIMS))))
    return lax.ppermute(array, AXES, pairs)


def inverse(target):
    table = {target(*source): source for source in np.ndindex(*DIMS)}
    return lambda *place: table[place]


def along_y(shift):
    return lambda y, zl, zh, x, c: ((y + shift) % 4, zl, zh, x, c)


def along_zl(shift):
    return lambda y, zl, zh, x, c: (y, (zl + shift) % 4, zh, x, c)


def to_plane(other_half):
    def target(y, zl, zh, x, c):
        column = zh * 8 + x * 2 + c
        plane, row = column % 4, column // 4
        return (y, plane, zh ^ other_half, ((row % 2) * 2 + plane // 2 + zl // 2) % 4, zl % 2)

    return target


def slot_of(r, k):
    y, zl, zh = (lax.axis_index(name) for name in ("y", "zl", "zh"))
    tokens = lax.rem(zl - r + 4, 4)
    row = lax.rem(y + k, 4)
    x = lax.rem(lax.rem(row, 2) * 2 + zl // 2 + tokens // 2, 4)
    other_half = jnp.where(row // 2 == zh, 0, 1)
    return (x * 2 + lax.rem(tokens, 2)) * 2 + other_half


def mixed_kernel(h0, h1, h2, h3, w0, w1, w2, w3, out, hs, ws, ob, h_sem, w_sem, o_sem):
    hidden, weights = (h0, h1, h2, h3), (w0, w1, w2, w3)
    for i in range(4):
        pltpu.make_async_copy(hidden[i], hs.at[i], h_sem.at[i]).start()
        pltpu.make_async_copy(weights[i], ws.at[i], w_sem.at[i]).start()
    for i in range(4):
        pltpu.make_async_copy(weights[i], ws.at[i], w_sem.at[i]).wait()
        pltpu.make_async_copy(hidden[i], hs.at[i], h_sem.at[i]).wait()

    def rows(r, _):
        block = hs[r].T

        def columns(k, _):
            ob[r * 4 + k] = jnp.dot(block, ws[k], preferred_element_type=jnp.float32).astype(jnp.bfloat16)
            pltpu.make_async_copy(ob.at[r * 4 + k], out.at[slot_of(r, k)], o_sem.at[r * 4 + k]).start()
            return 0

        return lax.fori_loop(0, 4, columns, 0)

    lax.fori_loop(0, 4, rows, 0)

    def finish(i, _):
        pltpu.make_async_copy(ob.at[i], out.at[i], o_sem.at[i]).wait()
        return 0

    lax.fori_loop(0, 16, finish, 0)


def weight_kernel(factor, h0, h1, h2, h3, u, o0, o1, o2, o3, hs, us, own, ob, h_sem, u_sem, o_sem):
    hidden, outs = (h0, h1, h2, h3), (o0, o1, o2, o3)
    t, d = us.shape[0] // 4, us.shape[1] // 4

    def piece(r, k):
        return pltpu.make_async_copy(
            u.at[slot_of(r, k)], us.at[pl.ds(r * t, t), pl.ds(k * d, d)], u_sem.at[r * 4 + k]
        )

    for i in range(4):
        pltpu.make_async_copy(hidden[i], hs.at[:, pl.ds(i * t, t)], h_sem.at[i]).start()
    for k in range(4):
        for r in range(4):
            piece(r, k).start()
    for i in range(4):
        pltpu.make_async_copy(hidden[i], hs.at[:, pl.ds(i * t, t)], h_sem.at[i]).wait()
    for k in (1, 2, 3, 0):
        for r in range(4):
            piece(r, k).wait()
        total = jnp.dot(hs[...], us[:, k * d : (k + 1) * d], preferred_element_type=jnp.float32) * factor
        if k == 0:
            own[...] = total
            pltpu.make_async_copy(own, outs[0], o_sem.at[0]).start()
        else:
            ob[k - 1] = total.astype(jnp.bfloat16)
            pltpu.make_async_copy(ob.at[k - 1], outs[k], o_sem.at[k]).start()
    pltpu.make_async_copy(own, outs[0], o_sem.at[0]).wait()
    for k in range(1, 4):
        pltpu.make_async_copy(ob.at[k - 1], outs[k], o_sem.at[k]).wait()


def hidden_kernel(w0, w1, w2, w3, u, o0, o1, o2, o3, ws, us, own, ob, w_sem, u_sem, o_sem):
    weights, outs = (w0, w1, w2, w3), (o0, o1, o2, o3)
    t, d = us.shape[0] // 4, us.shape[1] // 4

    def piece(r, k):
        return pltpu.make_async_copy(
            u.at[slot_of(r, k)], us.at[pl.ds(r * t, t), pl.ds(k * d, d)], u_sem.at[r * 4 + k]
        )

    for i in range(4):
        pltpu.make_async_copy(weights[i], ws.at[:, pl.ds(i * d, d)], w_sem.at[i]).start()
    for r in range(4):
        for k in range(4):
            piece(r, k).start()
    for i in range(4):
        pltpu.make_async_copy(weights[i], ws.at[:, pl.ds(i * d, d)], w_sem.at[i]).wait()
    for r in (1, 2, 3, 0):
        for k in range(4):
            piece(r, k).wait()
        total = lax.dot_general(
            ws[...], us[r * t : (r + 1) * t, :], (((1,), (1,)), ((), ())), preferred_element_type=jnp.float32
        )
        if r == 0:
            own[...] = total
            pltpu.make_async_copy(own, outs[0], o_sem.at[0]).start()
        else:
            ob[r - 1] = total.astype(jnp.bfloat16)
            pltpu.make_async_copy(ob.at[r - 1], outs[r], o_sem.at[r]).start()
    pltpu.make_async_copy(own, outs[0], o_sem.at[0]).wait()
    for r in range(1, 4):
        pltpu.make_async_copy(ob.at[r - 1], outs[r], o_sem.at[r]).wait()


def call(kernel, inputs, outputs, scratch, flops, name):
    moved = sum(v.size * v.dtype.itemsize for v in (*inputs, *outputs))
    return pl.pallas_call(
        kernel,
        out_shape=outputs,
        in_specs=[pl.BlockSpec(memory_space=pl.ANY)] * len(inputs),
        out_specs=[pl.BlockSpec(memory_space=pl.ANY)] * len(outputs),
        scratch_shapes=scratch,
        compiler_params=pltpu.CompilerParams(vmem_limit_bytes=VMEM_LIMIT),
        cost_estimate=pl.CostEstimate(flops=flops, bytes_accessed=moved, transcendentals=0),
        name=name,
    )(*inputs)


def local(hidden, codes, scales, upstream):
    t, f = hidden.shape
    d = codes.shape[1]
    factor = 1.0 / math.sqrt(t * 16)
    bf16, f32 = jnp.bfloat16, jnp.float32
    sem = pltpu.SemaphoreType.DMA
    shape = jax.ShapeDtypeStruct
    flops = 2 * f * 4 * t * 4 * d

    first = permute(upstream, to_plane(0))
    second = permute(upstream, to_plane(1))
    weight = (codes.astype(f32) * jnp.repeat(scales, BLOCK, axis=1)).astype(bf16)
    weights = [weight] + [permute(weight, along_y(-k)) for k in (1, 2, 3)]
    turned = hidden.T
    hiddens = [turned] + [permute(turned, along_zl(r)) for r in (1, 2, 3)]
    cots = lax.all_gather(jnp.stack([first, second]), ("x", "c"), axis=0, tiled=True)

    (terms,) = call(
        mixed_kernel,
        [*hiddens, *weights],
        [shape((16, t, d), bf16)],
        [
            pltpu.VMEM((4, f, t), bf16),
            pltpu.VMEM((4, f, d), bf16),
            pltpu.VMEM((16, t, d), bf16),
            sem((4,)),
            sem((4,)),
            sem((16,)),
        ],
        flops,
        "mixed_terms",
    )
    sums = lax.psum_scatter(terms, ("x", "c"), scatter_dimension=0, tiled=True)

    grads = call(
        functools.partial(weight_kernel, factor),
        [*hiddens, cots],
        [shape((f, d), f32)] + [shape((f, d), bf16)] * 3,
        [
            pltpu.VMEM((f, 4 * t), bf16),
            pltpu.VMEM((4 * t, 4 * d), bf16),
            pltpu.VMEM((f, d), f32),
            pltpu.VMEM((3, f, d), bf16),
            sem((4,)),
            sem((16,)),
            sem((4,)),
        ],
        flops,
        "weight_terms",
    )
    weight_parts = [permute(grads[k], along_y(k)) for k in (1, 2, 3)]
    backs = call(
        hidden_kernel,
        [*weights, cots],
        [shape((f, t), f32)] + [shape((f, t), bf16)] * 3,
        [
            pltpu.VMEM((f, 4 * d), bf16),
            pltpu.VMEM((4 * t, 4 * d), bf16),
            pltpu.VMEM((f, t), f32),
            pltpu.VMEM((3, f, t), bf16),
            sem((4,)),
            sem((16,)),
            sem((4,)),
        ],
        flops,
        "hidden_terms",
    )
    hidden_parts = [permute(backs[r], along_zl(-r)) for r in (1, 2, 3)]

    near = permute(sums[0], inverse(to_plane(0)))
    far = permute(sums[1], inverse(to_plane(1)))
    mixed = (near.astype(f32) + far.astype(f32)).astype(bf16)
    weight_grad = grads[0] + sum(part.astype(f32) for part in weight_parts)
    hidden_grad = (backs[0] + sum(part.astype(f32) for part in hidden_parts)).astype(bf16).T
    return (mixed, hidden_grad, weight_grad)


def solution(mesh):
    fine = Mesh(mesh.devices.reshape(DIMS), AXES)
    node, columns = ("y", "zl"), ("zh", "x", "c")
    return jax.shard_map(
        local,
        mesh=fine,
        in_specs=(P(node, columns), P(columns, node), P(columns, node), P(node, columns)),
        out_specs=(P(node, columns), P(node, columns), P(columns, node)),
        check_vma=False,
    )
```

```python
import functools
import math

import jax
import jax.numpy as jnp
from jax import lax
from jax.experimental import pallas as pl
from jax.experimental.pallas import tpu as pltpu
from jax.sharding import Mesh, PartitionSpec as P
import numpy as np

BLOCK = 256
AXES = ("y", "zl", "zh", "x", "c")
DIMS = (4, 4, 2, 4, 2)
VMEM_LIMIT = 50 * 1024 * 1024
bf16, f32 = jnp.bfloat16, jnp.float32

ORDERS = ((1, 3), (3, 1))


def permute(array, target):
    pairs = []
    for index, source in enumerate(np.ndindex(*DIMS)):
        place = target(*source)
        if place is not None:
            pairs.append((index, int(np.ravel_multi_index(place, DIMS))))
    return lax.ppermute(array, AXES, pairs)


def inverse(target):
    table = {target(*source): source for source in np.ndindex(*DIMS)}
    return lambda *place: table[place]


def partner(axis, mask):
    position = AXES.index(axis)

    def target(*place):
        return tuple(v ^ mask if i == position else v for i, v in enumerate(place))

    return target


def to_plane(kind):
    def target(y, zl, zh, x, c):
        column = zh * 8 + x * 2 + c
        plane, p, q = column % 4, column // 8, column // 4 % 2
        r = plane ^ zl
        return (y, plane, p ^ kind, 2 * (r // 2 ^ plane % 2 ^ plane // 2 ^ p) + (q ^ kind), r % 2)

    return target


def from_plane(kind, part):
    back = inverse(to_plane(kind))

    def target(y, zl, zh, x, c):
        if x // 2 ^ zl % 2 ^ zl // 2 ^ zh ^ kind != part:
            return None
        return back(y, zl, zh, x, c)

    return target


def place_of(kind, other, s):
    y, zl, zh, x, c = (lax.axis_index(name) for name in AXES)
    x, p = x ^ s, zh ^ kind
    r = 2 * ((x // 2) ^ (zl % 2) ^ (zl // 2) ^ p) + (c ^ other)
    return r, y ^ (2 * p + ((x % 2) ^ kind))


def step_for(part, k):
    y, zl, zh, x = (lax.axis_index(name) for name in ("y", "zl", "zh", "x"))
    p, q = (y ^ k) // 2, (y ^ k) % 2
    return x ^ (2 * (part ^ (zl % 2) ^ (zl // 2) ^ p) + (q ^ p ^ zh))


def gathered(own, near, rest, m, half, order):
    if m == 0:
        rows = own.shape[0] // 2
        return own.at[half * rows : (half + 1) * rows]
    if m == order[0]:
        return near
    return rest.at[0 if m == order[1] else 1]


def halves(refs, m):
    own, near0, rest0, near1, rest1 = refs
    return (
        gathered(own, near0, rest0, m, 0, ORDERS[0]),
        gathered(own, near1, rest1, m, 1, ORDERS[1]),
    )


def whole(refs, m):
    pair, rest = refs
    return (pair.at[0], pair.at[1], rest.at[1], rest.at[0])[m]


def upstream_copies(refs, us, u_sem, start):
    t, d = us.shape[0] // 4, us.shape[1] // 4
    for kind, (a, b) in enumerate(ORDERS):
        own, near, rest, pair, far = refs[5 * kind : 5 * kind + 5]
        pieces = (
            (own, 0, 0), (near, 0, a), (rest.at[0], 0, b), (rest.at[1], 0, 2),
            (pair.at[0], 1, 0), (pair.at[1], 1, a), (far.at[0], 1, b), (far.at[1], 1, 2),
        )
        for piece, other, s in pieces:
            r, k = place_of(kind, other, s)
            rows = pl.ds(pl.multiple_of(r * t, t), t)
            columns = pl.ds(pl.multiple_of(k * d, d), d)
            pltpu.make_async_copy(piece, us.at[rows, columns], u_sem.at[r * 4 + k]).start()


def wait_upstream(refs, us, u_sem, r, k):
    t, d = us.shape[0] // 4, us.shape[1] // 4
    place = us.at[r * t : (r + 1) * t, k * d : (k + 1) * d]
    pltpu.make_async_copy(refs[0], place, u_sem.at[r * 4 + k]).wait()


def mixed_kernel(part, *refs):
    hidden, weights = refs[:5], refs[5:7]
    send, keep, hs, ws, ob, h_sem, w_sem, o_sem = refs[7:]
    half, d = hs.shape[1] // 2, ob.shape[3]
    copies = []
    for m in range(4):
        place = ws.at[:, m * d : (m + 1) * d]
        copies.append(pltpu.make_async_copy(whole(weights, m), place, w_sem.at[m]))
    for m in range(2):
        for i, piece in enumerate(halves(hidden, 2 * part + m)):
            place = hs.at[m, i * half : (i + 1) * half]
            copies.append(pltpu.make_async_copy(piece, place, h_sem.at[2 * m + i]))
    for copy in copies:
        copy.start()
    for copy in copies:
        copy.wait()
    core = lax.axis_index("c")
    a, b = ORDERS[part]
    for i, out in enumerate((send, keep)):
        block = hs[core if i else 1 - core].T
        terms = jnp.dot(block, ws[...], preferred_element_type=f32).astype(bf16)
        for k in range(4):
            s = step_for(part, k)
            slot = jnp.where(s == 0, 0, jnp.where(s == b, 1, jnp.where(s == a, 2, 3)))
            ob[i, slot] = terms[:, k * d : (k + 1) * d]
        pltpu.make_async_copy(ob.at[i], out, o_sem.at[i]).start()
    for i, out in enumerate((send, keep)):
        pltpu.make_async_copy(ob.at[i], out, o_sem.at[i]).wait()


def give_out(total, m, orders, outs, own, ob, o_sem):
    half = total.shape[0] // 2
    copies = []
    for i, (a, b) in enumerate(orders):
        rows = slice(i * half, (i + 1) * half)
        mine, mid, send = outs[3 * i : 3 * i + 3]
        if m == 0:
            own[rows] = total[rows]
            copies.append(pltpu.make_async_copy(own.at[rows], mine, o_sem.at[m, i]))
        else:
            ob[m - 1, rows] = total[rows].astype(bf16)
            out = mid if m == b else send.at[0 if m == a else 1]
            copies.append(pltpu.make_async_copy(ob.at[m - 1, rows], out, o_sem.at[m, i]))
    for copy in copies:
        copy.start()
    return copies


def weight_kernel(factor, orders, *refs):
    hidden, cots, outs = refs[:5], refs[5:15], refs[15:21]
    hs, us, own, ob, h_sem, u_sem, o_sem = refs[21:]
    t, d = us.shape[0] // 4, us.shape[1] // 4
    half = hs.shape[0] // 2
    copies = []
    for m in range(4):
        for i, piece in enumerate(halves(hidden, m)):
            place = hs.at[i * half : (i + 1) * half, m * t : (m + 1) * t]
            copies.append(pltpu.make_async_copy(piece, place, h_sem.at[2 * m + i]))
    for copy in copies:
        copy.start()
    upstream_copies(cots, us, u_sem, True)
    for copy in copies:
        copy.wait()
    copies = []
    for k in (2, 1, 3, 0):
        for r in range(4):
            wait_upstream(cots, us, u_sem, r, k)
        total = jnp.dot(hs[...], us[:, k * d : (k + 1) * d], preferred_element_type=f32) * factor
        copies += give_out(total, k, orders, outs, own, ob, o_sem)
    for copy in copies:
        copy.wait()


def hidden_kernel(orders, *refs):
    weights, cots, outs = refs[:2], refs[2:12], refs[12:18]
    ws, us, own, ob, w_sem, u_sem, o_sem = refs[18:]
    t, d = us.shape[0] // 4, us.shape[1] // 4
    copies = []
    for m in range(4):
        place = ws.at[:, m * d : (m + 1) * d]
        copies.append(pltpu.make_async_copy(whole(weights, m), place, w_sem.at[m]))
    for copy in copies:
        copy.start()
    upstream_copies(cots, us, u_sem, True)
    for copy in copies:
        copy.wait()
    copies = []
    for r in (2, 1, 3, 0):
        for k in range(4):
            wait_upstream(cots, us, u_sem, r, k)
        total = lax.dot_general(
            ws[...], us[r * t : (r + 1) * t, :], (((1,), (1,)), ((), ())), preferred_element_type=f32
        )
        copies += give_out(total, r, orders, outs, own, ob, o_sem)
    for copy in copies:
        copy.wait()


def call(kernel, inputs, outputs, scratch, flops, name):
    moved = sum(v.size * v.dtype.itemsize for v in (*inputs, *outputs))
    return pl.pallas_call(
        kernel,
        out_shape=outputs,
        in_specs=[pl.BlockSpec(memory_space=pltpu.HBM)] * len(inputs),
        out_specs=[pl.BlockSpec(memory_space=pltpu.HBM)] * len(outputs),
        scratch_shapes=scratch,
        compiler_params=pltpu.CompilerParams(vmem_limit_bytes=VMEM_LIMIT),
        cost_estimate=pl.CostEstimate(flops=flops, bytes_accessed=moved, transcendentals=0),
        name=name,
    )(*inputs)


def after(value, *others):
    return lax.optimization_barrier((value, *others))[0]


def finish(parts, axis, order, first):
    mine, mid, _ = parts
    mid = (mid.astype(f32) + first[1].astype(f32)).astype(bf16)
    second = permute(mid, partner(axis, order[1]))
    return mine + first[0].astype(f32) + second.astype(f32)


def local(hidden, codes, scales, upstream):
    t, f = hidden.shape
    d = codes.shape[1]
    half = f // 2
    factor = 1.0 / math.sqrt(t * 16)
    sem = pltpu.SemaphoreType.DMA
    shape = jax.ShapeDtypeStruct
    flops = 2 * f * 4 * t * 4 * d

    owns = [permute(upstream, to_plane(kind)) for kind in (0, 1)]
    weight = (codes.astype(f32) * jnp.repeat(scales, BLOCK, axis=1)).astype(bf16)
    w_near = [permute(v, partner("y", 1)) for v in (weight[:half], weight[half:])]
    turned = after(hidden.T, *owns)
    h_own = [turned[:half], turned[half:]]
    h_near = [permute(v, partner("zl", a)) for v, (a, _) in zip(h_own, ORDERS)]
    u_near = [permute(v, partner("x", a)) for v, (a, _) in zip(owns, ORDERS)]
    h_rest = [
        permute(jnp.stack(pair), partner("zl", b)) for *pair, (_, b) in zip(h_own, h_near, ORDERS)
    ]
    u_pair = [jnp.stack(pair) for pair in zip(owns, u_near)]
    u_rest = [permute(pair, partner("x", b)) for pair, (_, b) in zip(u_pair, ORDERS)]
    w_pair = jnp.concatenate([weight, *w_near]).reshape(2, f, d)
    weights = [w_pair, permute(w_pair, partner("y", 3))]
    hiddens = [turned, h_near[0], h_rest[0], h_near[1], h_rest[1]]
    cots = []
    for kind in range(2):
        cots += [owns[kind], u_near[kind], u_rest[kind]]
        cots += [permute(v, partner("c", 1)) for v in (u_pair[kind], u_rest[kind])]

    def mixed_terms(part, *before):
        return call(
            functools.partial(mixed_kernel, part),
            [after(hiddens[0], *before), *hiddens[1:], *weights],
            [shape((4, t, d), bf16)] * 2,
            [
                pltpu.VMEM((2, f, t), bf16),
                pltpu.VMEM((f, 4 * d), bf16),
                pltpu.VMEM((2, 4, t, d), bf16),
                sem((4,)),
                sem((4,)),
                sem((2,)),
            ],
            flops // 2,
            "mixed_terms",
        )

    def give(part, keep, got):
        share = (keep[2:].astype(f32) + got[2:].astype(f32)).astype(bf16)
        return share, permute(share, partner("x", ORDERS[part][0]))

    def take(part, keep, got, first, *before):
        mid = (keep[1].astype(f32) + got[1].astype(f32) + first[1].astype(f32)).astype(bf16)
        second = permute(after(mid, *before), partner("x", ORDERS[part][1]))
        total = keep[0].astype(f32) + got[0].astype(f32) + first[0].astype(f32) + second.astype(f32)
        return second, [permute(total.astype(bf16), from_plane(kind, part)) for kind in (0, 1)]

    send0, keep0 = mixed_terms(0, *u_rest)
    got0 = permute(send0, partner("c", 1))
    share0, first0 = give(0, keep0, got0)
    send1, keep1 = mixed_terms(1, send0)
    got1 = permute(send1, partner("c", 1))
    share1, first1 = give(1, keep1, got1)
    orders = ORDERS[::-1]
    backs = call(
        functools.partial(hidden_kernel, orders),
        [after(weights[0], send1, share0), *weights[1:], *cots],
        [shape((half, t), f32), shape((half, t), bf16), shape((2, half, t), bf16)] * 2,
        [
            pltpu.VMEM((f, 4 * d), bf16),
            pltpu.VMEM((4 * t, 4 * d), bf16),
            pltpu.VMEM((f, t), f32),
            pltpu.VMEM((3, f, t), bf16),
            sem((4,)),
            sem((16,)),
            sem((4, 2)),
        ],
        flops,
        "hidden_terms",
    )
    sent = [permute(backs[3 * i + 2], partner("zl", orders[i][0])) for i in range(2)]
    grads = call(
        functools.partial(weight_kernel, factor, orders),
        [after(hiddens[0], backs[2], share1), *hiddens[1:], *cots],
        [shape((half, d), f32), shape((half, d), bf16), shape((2, half, d), bf16)] * 2,
        [
            pltpu.VMEM((f, 4 * t), bf16),
            pltpu.VMEM((4 * t, 4 * d), bf16),
            pltpu.VMEM((f, d), f32),
            pltpu.VMEM((3, f, d), bf16),
            sem((8,)),
            sem((16,)),
            sem((4, 2)),
        ],
        flops,
        "weight_terms",
    )
    first0, first1, *sent = lax.optimization_barrier((first0, first1, *sent, grads[2]))[:4]
    second0, ends = take(0, keep0, got0, first0)
    back = [finish(backs[3 * i : 3 * i + 3], "zl", orders[i], sent[i]) for i in range(2)]
    second1, more = take(1, keep1, got1, first1)
    ends += more
    grad = []
    for i in range(2):
        send = after(grads[3 * i + 2], first0, first1, *sent)
        first = permute(send, partner("y", orders[i][0]))
        grad.append(finish(grads[3 * i : 3 * i + 3], "y", orders[i], first))
    mixed = sum(v.astype(f32) for v in ends).astype(bf16)
    hidden_grad = jnp.concatenate(back).astype(bf16).T
    return (mixed, hidden_grad, jnp.concatenate(grad))


def solution(mesh):
    fine = Mesh(mesh.devices.reshape(DIMS), AXES)
    node, columns = ("y", "zl"), ("zh", "x", "c")
    return jax.shard_map(
        local,
        mesh=fine,
        in_specs=(P(node, columns), P(columns, node), P(columns, node), P(node, columns)),
        out_specs=(P(node, columns), P(node, columns), P(columns, node)),
        check_vma=False,
    )
```

```python
import functools
import math

import jax
import jax.numpy as jnp
from jax import lax
from jax.experimental import pallas as pl
from jax.experimental.pallas import tpu as pltpu
from jax.sharding import Mesh, PartitionSpec as P
import numpy as np

BLOCK = 256
AXES = ("y", "zl", "zh", "x", "c")
DIMS = (4, 4, 2, 4, 2)
VMEM_LIMIT = 50 * 1024 * 1024
bf16, f32 = jnp.bfloat16, jnp.float32

ORDERS = ((1, 3), (3, 1))


def permute(array, target):
    pairs = []
    for index, source in enumerate(np.ndindex(*DIMS)):
        place = target(*source)
        if place is not None:
            pairs.append((index, int(np.ravel_multi_index(place, DIMS))))
    return lax.ppermute(array, AXES, pairs)


def inverse(target):
    table = {target(*source): source for source in np.ndindex(*DIMS)}
    return lambda *place: table[place]


def partner(axis, mask):
    position = AXES.index(axis)

    def target(*place):
        return tuple(v ^ mask if i == position else v for i, v in enumerate(place))

    return target


def to_plane(kind):
    def target(y, zl, zh, x, c):
        column = zh * 8 + x * 2 + c
        plane, p, q = column % 4, column // 8, column // 4 % 2
        r = plane ^ zl
        return (y, plane, p ^ 1 - kind, 2 * (r // 2 ^ plane % 2 ^ plane // 2 ^ p) + (q ^ 1 - kind), r % 2)

    return target


def place_of(kind, other, s):
    y, zl, zh, x, c = (lax.axis_index(name) for name in AXES)
    x, p = x ^ s, zh ^ 1 - kind
    r = 2 * ((x // 2) ^ (zl % 2) ^ (zl // 2) ^ p) + (c ^ other)
    return r, y ^ (2 * p + ((x % 2) ^ 1 - kind))


def step_for(part, k):
    y, zl, zh, x = (lax.axis_index(name) for name in ("y", "zl", "zh", "x"))
    p, q = (y ^ k) // 2, (y ^ k) % 2
    return x ^ (2 * (part ^ (zl % 2) ^ (zl // 2) ^ p) + (q ^ p ^ zh))


def gathered(own, near, rest, m, half, order):
    if m == 0:
        rows = own.shape[0] // 2
        return own.at[half * rows : (half + 1) * rows]
    if m == order[0]:
        return near
    return rest.at[0 if m == order[1] else 1]


def halves(refs, m):
    own, near0, rest0, near1, rest1 = refs
    return (
        gathered(own, near0, rest0, m, 0, ORDERS[0]),
        gathered(own, near1, rest1, m, 1, ORDERS[1]),
    )


def whole(refs, m):
    pair, rest = refs
    return (pair.at[0], pair.at[1], rest.at[1], rest.at[0])[m]


def upstream_copies(refs, us, u_sem, start):
    t, d = us.shape[0] // 4, us.shape[1] // 4
    for kind, (a, b) in enumerate(ORDERS):
        own, near, rest, pair, far = refs[5 * kind : 5 * kind + 5]
        pieces = (
            (own, 0, 0), (near, 0, a), (rest.at[0], 0, b), (rest.at[1], 0, 2),
            (pair.at[0], 1, 0), (pair.at[1], 1, a), (far.at[0], 1, b), (far.at[1], 1, 2),
        )
        for piece, other, s in pieces:
            r, k = place_of(kind, other, s)
            rows = pl.ds(pl.multiple_of(r * t, t), t)
            columns = pl.ds(pl.multiple_of(k * d, d), d)
            pltpu.make_async_copy(piece, us.at[rows, columns], u_sem.at[r * 4 + k]).start()


def wait_upstream(refs, us, u_sem, r, k):
    t, d = us.shape[0] // 4, us.shape[1] // 4
    place = us.at[r * t : (r + 1) * t, k * d : (k + 1) * d]
    pltpu.make_async_copy(refs[0], place, u_sem.at[r * 4 + k]).wait()


def mixed_kernel(part, *refs):
    hidden, weights = refs[:5], refs[5:7]
    send, keep, hs, ws, ob, h_sem, w_sem, o_sem = refs[7:]
    half, d = hs.shape[1] // 2, ob.shape[3]
    copies = []
    for m in range(4):
        place = ws.at[:, m * d : (m + 1) * d]
        copies.append(pltpu.make_async_copy(whole(weights, m), place, w_sem.at[m]))
    for m in range(2):
        for i, piece in enumerate(halves(hidden, 2 * part + m)):
            place = hs.at[m, i * half : (i + 1) * half]
            copies.append(pltpu.make_async_copy(piece, place, h_sem.at[2 * m + i]))
    for copy in copies:
        copy.start()
    for copy in copies:
        copy.wait()
    core = lax.axis_index("c")
    a, b = ORDERS[part]
    for i, out in enumerate((send, keep)):
        block = hs[core if i else 1 - core].T
        terms = jnp.dot(block, ws[...], preferred_element_type=f32).astype(bf16)
        for k in range(4):
            s = step_for(part, k)
            slot = jnp.where(s == 0, 0, jnp.where(s == b, 1, jnp.where(s == a, 2, 3)))
            ob[i, slot] = terms[:, k * d : (k + 1) * d]
        pltpu.make_async_copy(ob.at[i], out, o_sem.at[i]).start()
    for i, out in enumerate((send, keep)):
        pltpu.make_async_copy(ob.at[i], out, o_sem.at[i]).wait()


def give_out(total, m, orders, outs, own, ob, o_sem):
    half = total.shape[0] // 2
    copies = []
    for i, (a, b) in enumerate(orders):
        rows = slice(i * half, (i + 1) * half)
        mine, mid, send = outs[3 * i : 3 * i + 3]
        if m == 0:
            own[rows] = total[rows]
            copies.append(pltpu.make_async_copy(own.at[rows], mine, o_sem.at[m, i]))
        else:
            ob[m - 1, rows] = total[rows].astype(bf16)
            out = mid if m == b else send.at[0 if m == a else 1]
            copies.append(pltpu.make_async_copy(ob.at[m - 1, rows], out, o_sem.at[m, i]))
    for copy in copies:
        copy.start()
    return copies


def weight_kernel(factor, orders, *refs):
    hidden, cots, outs = refs[:5], refs[5:15], refs[15:21]
    hs, us, own, ob, h_sem, u_sem, o_sem = refs[21:]
    t, d = us.shape[0] // 4, us.shape[1] // 4
    half = hs.shape[0] // 2
    copies = []
    for m in range(4):
        for i, piece in enumerate(halves(hidden, m)):
            place = hs.at[i * half : (i + 1) * half, m * t : (m + 1) * t]
            copies.append(pltpu.make_async_copy(piece, place, h_sem.at[2 * m + i]))
    for copy in copies:
        copy.start()
    upstream_copies(cots, us, u_sem, True)
    for copy in copies:
        copy.wait()
    copies = []
    for k in (2, 1, 3, 0):
        for r in range(4):
            wait_upstream(cots, us, u_sem, r, k)
        total = jnp.dot(hs[...], us[:, k * d : (k + 1) * d], preferred_element_type=f32) * factor
        copies += give_out(total, k, orders, outs, own, ob, o_sem)
    for copy in copies:
        copy.wait()


def hidden_kernel(orders, *refs):
    weights, cots, outs = refs[:2], refs[2:12], refs[12:18]
    ws, us, own, ob, w_sem, u_sem, o_sem = refs[18:]
    t, d = us.shape[0] // 4, us.shape[1] // 4
    copies = []
    for m in range(4):
        place = ws.at[:, m * d : (m + 1) * d]
        copies.append(pltpu.make_async_copy(whole(weights, m), place, w_sem.at[m]))
    for copy in copies:
        copy.start()
    upstream_copies(cots, us, u_sem, True)
    for copy in copies:
        copy.wait()
    copies = []
    for r in (2, 1, 3, 0):
        for k in range(4):
            wait_upstream(cots, us, u_sem, r, k)
        total = lax.dot_general(
            ws[...], us[r * t : (r + 1) * t, :], (((1,), (1,)), ((), ())), preferred_element_type=f32
        )
        copies += give_out(total, r, orders, outs, own, ob, o_sem)
    for copy in copies:
        copy.wait()


def call(kernel, inputs, outputs, scratch, flops, name):
    moved = sum(v.size * v.dtype.itemsize for v in (*inputs, *outputs))
    return pl.pallas_call(
        kernel,
        out_shape=outputs,
        in_specs=[pl.BlockSpec(memory_space=pltpu.HBM)] * len(inputs),
        out_specs=[pl.BlockSpec(memory_space=pltpu.HBM)] * len(outputs),
        scratch_shapes=scratch,
        compiler_params=pltpu.CompilerParams(vmem_limit_bytes=VMEM_LIMIT),
        cost_estimate=pl.CostEstimate(flops=flops, bytes_accessed=moved, transcendentals=0),
        name=name,
    )(*inputs)


def after(value, *others):
    return lax.optimization_barrier((value, *others))[0]


def finish(parts, axis, order, first, mids, *before):
    mine, mid, _ = parts
    mid = (mid.astype(f32) + first[1].astype(f32)).astype(bf16)
    mid = after(mid, *before)
    mids.append(mid)
    second = permute(mid, partner(axis, order[1]))
    return mine + first[0].astype(f32) + second.astype(f32)


def local(hidden, codes, scales, upstream):
    t, f = hidden.shape
    d = codes.shape[1]
    half = f // 2
    factor = 1.0 / math.sqrt(t * 16)
    sem = pltpu.SemaphoreType.DMA
    shape = jax.ShapeDtypeStruct
    flops = 2 * f * 4 * t * 4 * d

    owns = [permute(upstream, to_plane(kind)) for kind in (0, 1)]
    weight = (codes.astype(f32) * jnp.repeat(scales, BLOCK, axis=1)).astype(bf16)
    w_near = [permute(v, partner("y", 1)) for v in (weight[:half], weight[half:])]
    turned = after(hidden.T, *owns)
    h_own = [turned[:half], turned[half:]]
    h_near = [permute(v, partner("zl", a)) for v, (a, _) in zip(h_own, ORDERS)]
    u_near = [permute(v, partner("x", a)) for v, (a, _) in zip(owns, ORDERS)]
    h_rest = [
        permute(jnp.stack(pair), partner("zl", b)) for *pair, (_, b) in zip(h_own, h_near, ORDERS)
    ]
    u_pair = [jnp.stack(pair) for pair in zip(owns, u_near)]
    u_rest = [permute(pair, partner("x", b)) for pair, (_, b) in zip(u_pair, ORDERS)]
    w_pair = jnp.concatenate([weight, *w_near]).reshape(2, f, d)
    weights = [w_pair, permute(w_pair, partner("y", 3))]
    hiddens = [turned, h_near[0], h_rest[0], h_near[1], h_rest[1]]
    cots = []
    for kind in range(2):
        cots += [owns[kind], u_near[kind], u_rest[kind]]
        cots += [permute(v, partner("c", 1)) for v in (u_pair[kind], u_rest[kind])]

    def mixed_terms(part, *before):
        return call(
            functools.partial(mixed_kernel, part),
            [after(hiddens[0], *before), *hiddens[1:], *weights],
            [shape((4, t, d), bf16)] * 2,
            [
                pltpu.VMEM((2, f, t), bf16),
                pltpu.VMEM((f, 4 * d), bf16),
                pltpu.VMEM((2, 4, t, d), bf16),
                sem((4,)),
                sem((4,)),
                sem((2,)),
            ],
            flops // 2,
            "mixed_terms",
        )

    def give(part, keep, got):
        share = (keep[2:].astype(f32) + got[2:].astype(f32)).astype(bf16)
        return share, permute(share, partner("x", ORDERS[part][0]))

    def pass_on(part, keep, got, first):
        mid = (keep[1].astype(f32) + got[1].astype(f32) + first[1].astype(f32)).astype(bf16)
        return mid, permute(mid, partner("x", ORDERS[part][1]))

    def total(keep, got, first, second):
        parts = (keep[0], got[0], first[0], second)
        return sum(v.astype(f32) for v in parts).astype(bf16)

    send0, keep0 = mixed_terms(0, *u_rest)
    got0 = permute(send0, partner("c", 1))
    share0, first0 = give(0, keep0, got0)
    send1, keep1 = mixed_terms(1, send0)
    got1 = permute(after(send1, got0), partner("c", 1))
    share1, first1 = give(1, keep1, got1)
    orders = ORDERS[::-1]
    backs = call(
        functools.partial(hidden_kernel, orders),
        [after(weights[0], send1, share0), *weights[1:], *cots],
        [shape((half, t), f32), shape((half, t), bf16), shape((2, half, t), bf16)] * 2,
        [
            pltpu.VMEM((f, 4 * d), bf16),
            pltpu.VMEM((4 * t, 4 * d), bf16),
            pltpu.VMEM((f, t), f32),
            pltpu.VMEM((3, f, t), bf16),
            sem((4,)),
            sem((16,)),
            sem((4, 2)),
        ],
        flops,
        "hidden_terms",
    )
    sent = [permute(backs[3 * i + 2], partner("zl", orders[i][0])) for i in range(2)]
    mid0, second0 = pass_on(0, keep0, got0, first0)
    mid1, second1 = pass_on(1, keep1, got1, first1)
    grads = call(
        functools.partial(weight_kernel, factor, orders),
        [after(hiddens[0], backs[2], mid0, mid1), *hiddens[1:], *cots],
        [shape((half, d), f32), shape((half, d), bf16), shape((2, half, d), bf16)] * 2,
        [
            pltpu.VMEM((f, 4 * t), bf16),
            pltpu.VMEM((4 * t, 4 * d), bf16),
            pltpu.VMEM((f, d), f32),
            pltpu.VMEM((3, f, d), bf16),
            sem((8,)),
            sem((16,)),
            sem((4, 2)),
        ],
        flops,
        "weight_terms",
    )
    second0, second1 = lax.optimization_barrier((second0, second1, grads[2]))[:2]
    others = [
        permute(after(grads[3 * i + 2], second0, second1), partner("y", orders[i][0])) for i in range(2)
    ]
    totals = [total(keep0, got0, first0, second0), total(keep1, got1, first1, second1)]
    zl, zh, x = (lax.axis_index(name) for name in ("zl", "zh", "x"))
    swap = (x // 2 ^ zl % 2 ^ zl // 2 ^ zh) == 0
    kinds = (jnp.where(swap, totals[1], totals[0]), jnp.where(swap, totals[0], totals[1]))
    ends = [permute(v, inverse(to_plane(kind))) for kind, v in enumerate(kinds)]
    sent = [after(v, *kinds) for v in sent]
    before = ([], others[:1])
    mids = []
    back = [
        finish(backs[3 * i : 3 * i + 3], "zl", orders[i], sent[i], mids, *before[i]) for i in range(2)
    ]
    grad = [finish(grads[3 * i : 3 * i + 3], "y", orders[i], others[i], mids) for i in range(2)]
    ends = lax.optimization_barrier((*ends, *mids[1:]))[:2]
    mixed = (ends[0].astype(f32) + ends[1].astype(f32)).astype(bf16)
    hidden_grad = jnp.concatenate(back).astype(bf16).T
    return (mixed, hidden_grad, jnp.concatenate(grad))


def solution(mesh):
    fine = Mesh(mesh.devices.reshape(DIMS), AXES)
    node, columns = ("y", "zl"), ("zh", "x", "c")
    return jax.shard_map(
        local,
        mesh=fine,
        in_specs=(P(node, columns), P(columns, node), P(columns, node), P(node, columns)),
        out_specs=(P(node, columns), P(node, columns), P(columns, node)),
        check_vma=False,
    )
```

```python
import functools
import math

import jax
import jax.numpy as jnp
from jax import lax
from jax.experimental import pallas as pl
from jax.experimental.pallas import tpu as pltpu
from jax.sharding import Mesh, PartitionSpec as P
import numpy as np

BLOCK = 256
AXES = ("y", "zl", "zh", "x", "c")
DIMS = (4, 4, 2, 4, 2)
VMEM_LIMIT = 60 * 1024 * 1024
bf16, f32 = jnp.bfloat16, jnp.float32

ORDERS = ((1, 3), (3, 1))


def permute(array, target):
    pairs = []
    for index, source in enumerate(np.ndindex(*DIMS)):
        place = target(*source)
        if place is not None:
            pairs.append((index, int(np.ravel_multi_index(place, DIMS))))
    return lax.ppermute(array, AXES, pairs)


def inverse(target):
    table = {target(*source): source for source in np.ndindex(*DIMS)}
    return lambda *place: table[place]


def partner(axis, mask):
    position = AXES.index(axis)

    def target(*place):
        return tuple(v ^ mask if i == position else v for i, v in enumerate(place))

    return target


def to_plane(kind):
    def target(y, zl, zh, x, c):
        column = zh * 8 + x * 2 + c
        plane, p, q = column % 4, column // 8, column // 4 % 2
        r = plane ^ zl
        return (y, plane, p ^ 1 - kind, 2 * (r // 2 ^ plane % 2 ^ plane // 2 ^ p) + (q ^ 1 - kind), r % 2)

    return target


def place_of(kind, other, s):
    y, zl, zh, x, c = (lax.axis_index(name) for name in AXES)
    x, p = x ^ s, zh ^ 1 - kind
    r = 2 * ((x // 2) ^ (zl % 2) ^ (zl // 2) ^ p) + (c ^ other)
    return r, y ^ (2 * p + ((x % 2) ^ 1 - kind))


def step_for(part, k):
    y, zl, zh, x = (lax.axis_index(name) for name in ("y", "zl", "zh", "x"))
    p, q = (y ^ k) // 2, (y ^ k) % 2
    return x ^ (2 * (part ^ (zl % 2) ^ (zl // 2) ^ p) + (q ^ p ^ zh))


def gathered(own, near, rest, m, half, order):
    if m == 0:
        rows = own.shape[0] // 2
        return own.at[half * rows : (half + 1) * rows]
    if m == order[0]:
        return near
    return rest.at[0 if m == order[1] else 1]


def halves(refs, m):
    own, near0, rest0, near1, rest1 = refs
    return (
        gathered(own, near0, rest0, m, 0, ORDERS[0]),
        gathered(own, near1, rest1, m, 1, ORDERS[1]),
    )


def whole(refs, m):
    pair, rest = refs
    return (pair.at[0], pair.at[1], rest.at[1], rest.at[0])[m]


def upstream_copies(refs, us, u_sem, start):
    t, d = us.shape[0] // 4, us.shape[1] // 4
    for kind, (a, b) in enumerate(ORDERS):
        own, near, rest, pair, far = refs[5 * kind : 5 * kind + 5]
        pieces = (
            (own, 0, 0), (near, 0, a), (rest.at[0], 0, b), (rest.at[1], 0, 2),
            (pair.at[0], 1, 0), (pair.at[1], 1, a), (far.at[0], 1, b), (far.at[1], 1, 2),
        )
        for piece, other, s in pieces:
            r, k = place_of(kind, other, s)
            rows = pl.ds(pl.multiple_of(r * t, t), t)
            columns = pl.ds(pl.multiple_of(k * d, d), d)
            pltpu.make_async_copy(piece, us.at[rows, columns], u_sem.at[r * 4 + k]).start()


def wait_upstream(refs, us, u_sem, r, k):
    t, d = us.shape[0] // 4, us.shape[1] // 4
    place = us.at[r * t : (r + 1) * t, k * d : (k + 1) * d]
    pltpu.make_async_copy(refs[0], place, u_sem.at[r * 4 + k]).wait()


def mixed_kernel(part, *refs):
    hidden, weights = refs[:5], refs[5:7]
    send, keep, hs, ws, ob, h_sem, w_sem, o_sem = refs[7:]
    half, d = hs.shape[1] // 2, ob.shape[3]
    copies = []
    for m in range(4):
        place = ws.at[:, m * d : (m + 1) * d]
        copies.append(pltpu.make_async_copy(whole(weights, m), place, w_sem.at[m]))
    for m in range(2):
        for i, piece in enumerate(halves(hidden, 2 * part + m)):
            place = hs.at[m, i * half : (i + 1) * half]
            copies.append(pltpu.make_async_copy(piece, place, h_sem.at[2 * m + i]))
    for copy in copies:
        copy.start()
    for copy in copies:
        copy.wait()
    core = lax.axis_index("c")
    a, b = ORDERS[part]
    for i, out in enumerate((send, keep)):
        block = hs[core if i else 1 - core].T
        terms = jnp.dot(block, ws[...], preferred_element_type=f32).astype(bf16)
        for k in range(4):
            s = step_for(part, k)
            slot = jnp.where(s == 0, 0, jnp.where(s == b, 1, jnp.where(s == a, 2, 3)))
            ob[i, slot] = terms[:, k * d : (k + 1) * d]
        pltpu.make_async_copy(ob.at[i], out, o_sem.at[i]).start()
    for i, out in enumerate((send, keep)):
        pltpu.make_async_copy(ob.at[i], out, o_sem.at[i]).wait()


def give_out(total, m, orders, outs, own, ob, o_sem):
    half = total.shape[0] // 2
    copies = []
    for i, (a, b) in enumerate(orders):
        rows = slice(i * half, (i + 1) * half)
        mine, mid, send = outs[3 * i : 3 * i + 3]
        if m == 0:
            own[rows] = total[rows]
            copies.append(pltpu.make_async_copy(own.at[rows], mine, o_sem.at[m, i]))
        else:
            ob[m - 1, rows] = total[rows].astype(bf16)
            out = mid if m == b else send.at[0 if m == a else 1]
            copies.append(pltpu.make_async_copy(ob.at[m - 1, rows], out, o_sem.at[m, i]))
    for copy in copies:
        copy.start()
    return copies


def weight_kernel(factor, orders, *refs):
    hidden, cots, outs = refs[:5], refs[5:15], refs[15:21]
    hs, us, own, ob, h_sem, u_sem, o_sem = refs[21:]
    t, d = us.shape[0] // 4, us.shape[1] // 4
    half = hs.shape[0] // 2
    copies = []
    for m in range(4):
        for i, piece in enumerate(halves(hidden, m)):
            place = hs.at[i * half : (i + 1) * half, m * t : (m + 1) * t]
            copies.append(pltpu.make_async_copy(piece, place, h_sem.at[2 * m + i]))
    for copy in copies:
        copy.start()
    upstream_copies(cots, us, u_sem, True)
    for copy in copies:
        copy.wait()
    copies = []
    for k in (2, 1, 3, 0):
        for r in range(4):
            wait_upstream(cots, us, u_sem, r, k)
        total = jnp.dot(hs[...], us[:, k * d : (k + 1) * d], preferred_element_type=f32) * factor
        copies += give_out(total, k, orders, outs, own, ob, o_sem)
    for copy in copies:
        copy.wait()


def hidden_kernel(orders, *refs):
    weights, cots, outs = refs[:2], refs[2:12], refs[12:18]
    ws, us, own, ob, w_sem, u_sem, o_sem = refs[18:]
    t, d = us.shape[0] // 4, us.shape[1] // 4
    copies = []
    for m in range(4):
        place = ws.at[:, m * d : (m + 1) * d]
        copies.append(pltpu.make_async_copy(whole(weights, m), place, w_sem.at[m]))
    for copy in copies:
        copy.start()
    upstream_copies(cots, us, u_sem, True)
    for copy in copies:
        copy.wait()
    copies = []
    for r in (2, 1, 3, 0):
        for k in range(4):
            wait_upstream(cots, us, u_sem, r, k)
        total = lax.dot_general(
            ws[...], us[r * t : (r + 1) * t, :], (((1,), (1,)), ((), ())), preferred_element_type=f32
        )
        copies += give_out(total, r, orders, outs, own, ob, o_sem)
    for copy in copies:
        copy.wait()


def call(kernel, inputs, outputs, scratch, flops, name):
    moved = sum(v.size * v.dtype.itemsize for v in (*inputs, *outputs))
    return pl.pallas_call(
        kernel,
        out_shape=outputs,
        in_specs=[pl.BlockSpec(memory_space=pltpu.HBM)] * len(inputs),
        out_specs=[pl.BlockSpec(memory_space=pltpu.HBM)] * len(outputs),
        scratch_shapes=scratch,
        compiler_params=pltpu.CompilerParams(vmem_limit_bytes=VMEM_LIMIT),
        cost_estimate=pl.CostEstimate(flops=flops, bytes_accessed=moved, transcendentals=0),
        name=name,
    )(*inputs)


def after(value, *others):
    return lax.optimization_barrier((value, *others))[0]


def finish(parts, axis, order, first, mids, *before):
    mine, mid, _ = parts
    mid = (mid.astype(f32) + first[1].astype(f32)).astype(bf16)
    mid = after(mid, *before)
    mids.append(mid)
    second = permute(mid, partner(axis, order[1]))
    return mine + first[0].astype(f32) + second.astype(f32)


def local(hidden, codes, scales, upstream):
    t, f = hidden.shape
    d = codes.shape[1]
    half = f // 2
    factor = 1.0 / math.sqrt(t * 16)
    sem = pltpu.SemaphoreType.DMA
    shape = jax.ShapeDtypeStruct
    flops = 2 * f * 4 * t * 4 * d

    owns = [permute(upstream, to_plane(kind)) for kind in (0, 1)]
    weight = (codes.astype(f32) * jnp.repeat(scales, BLOCK, axis=1)).astype(bf16)
    w_near = [permute(v, partner("y", 1)) for v in (weight[:half], weight[half:])]
    turned = after(hidden.T, *owns)
    h_own = [turned[:half], turned[half:]]
    h_near = [permute(v, partner("zl", a)) for v, (a, _) in zip(h_own, ORDERS)]
    u_near = [permute(v, partner("x", a)) for v, (a, _) in zip(owns, ORDERS)]
    h_rest = [
        permute(jnp.stack(pair), partner("zl", b)) for *pair, (_, b) in zip(h_own, h_near, ORDERS)
    ]
    u_pair = [jnp.stack(pair) for pair in zip(owns, u_near)]
    u_rest = [permute(pair, partner("x", b)) for pair, (_, b) in zip(u_pair, ORDERS)]
    w_pair = jnp.concatenate([weight, *w_near]).reshape(2, f, d)
    weights = [w_pair, permute(w_pair, partner("y", 3))]
    hiddens = [turned, h_near[0], h_rest[0], h_near[1], h_rest[1]]
    cots = []
    for kind in range(2):
        cots += [owns[kind], u_near[kind], u_rest[kind]]
        cots += [permute(v, partner("c", 1)) for v in (u_pair[kind], u_rest[kind])]

    def mixed_terms(part, *before):
        return call(
            functools.partial(mixed_kernel, part),
            [after(hiddens[0], *before), *hiddens[1:], *weights],
            [shape((4, t, d), bf16)] * 2,
            [
                pltpu.VMEM((2, f, t), bf16),
                pltpu.VMEM((f, 4 * d), bf16),
                pltpu.VMEM((2, 4, t, d), bf16),
                sem((4,)),
                sem((4,)),
                sem((2,)),
            ],
            flops // 2,
            "mixed_terms",
        )

    def give(part, keep, got):
        share = (keep[2:].astype(f32) + got[2:].astype(f32)).astype(bf16)
        return share, permute(share, partner("x", ORDERS[part][0]))

    def pass_on(part, keep, got, first):
        mid = (keep[1].astype(f32) + got[1].astype(f32) + first[1].astype(f32)).astype(bf16)
        return mid, permute(mid, partner("x", ORDERS[part][1]))

    def total(keep, got, first, second):
        parts = (keep[0], got[0], first[0], second)
        return sum(v.astype(f32) for v in parts).astype(bf16)

    send0, keep0 = mixed_terms(0, *u_rest)
    got0 = permute(send0, partner("c", 1))
    share0, first0 = give(0, keep0, got0)
    send1, keep1 = mixed_terms(1, send0)
    got1 = permute(after(send1, got0), partner("c", 1))
    share1, first1 = give(1, keep1, got1)
    orders = ORDERS[::-1]
    backs = call(
        functools.partial(hidden_kernel, orders),
        [after(weights[0], send1, share0), *weights[1:], *cots],
        [shape((half, t), f32), shape((half, t), bf16), shape((2, half, t), bf16)] * 2,
        [
            pltpu.VMEM((f, 4 * d), bf16),
            pltpu.VMEM((4 * t, 4 * d), bf16),
            pltpu.VMEM((f, t), f32),
            pltpu.VMEM((3, f, t), bf16),
            sem((4,)),
            sem((16,)),
            sem((4, 2)),
        ],
        flops,
        "hidden_terms",
    )
    sent = [permute(backs[3 * i + 2], partner("zl", orders[i][0])) for i in range(2)]
    mid0, second0 = pass_on(0, keep0, got0, first0)
    mid1, second1 = pass_on(1, keep1, got1, first1)
    grads = call(
        functools.partial(weight_kernel, factor, orders),
        [after(hiddens[0], backs[2], mid0, mid1), *hiddens[1:], *cots],
        [shape((half, d), f32), shape((half, d), bf16), shape((2, half, d), bf16)] * 2,
        [
            pltpu.VMEM((f, 4 * t), bf16),
            pltpu.VMEM((4 * t, 4 * d), bf16),
            pltpu.VMEM((f, d), f32),
            pltpu.VMEM((3, f, d), bf16),
            sem((8,)),
            sem((16,)),
            sem((4, 2)),
        ],
        flops,
        "weight_terms",
    )
    second0, second1 = lax.optimization_barrier((second0, second1, grads[2]))[:2]
    others = [
        permute(after(grads[3 * i + 2], second0, second1), partner("y", orders[i][0])) for i in range(2)
    ]
    totals = [total(keep0, got0, first0, second0), total(keep1, got1, first1, second1)]
    zl, zh, x = (lax.axis_index(name) for name in ("zl", "zh", "x"))
    swap = (x // 2 ^ zl % 2 ^ zl // 2 ^ zh) == 0
    kinds = (jnp.where(swap, totals[1], totals[0]), jnp.where(swap, totals[0], totals[1]))
    ends = [permute(v, inverse(to_plane(kind))) for kind, v in enumerate(kinds)]
    sent = [after(v, *kinds) for v in sent]
    before = ([], others[:1])
    mids = []
    back = [
        finish(backs[3 * i : 3 * i + 3], "zl", orders[i], sent[i], mids, *before[i]) for i in range(2)
    ]
    grad = [finish(grads[3 * i : 3 * i + 3], "y", orders[i], others[i], mids) for i in range(2)]
    ends = lax.optimization_barrier((*ends, *mids[1:]))[:2]
    mixed = (ends[0].astype(f32) + ends[1].astype(f32)).astype(bf16)
    hidden_grad = jnp.concatenate(back).astype(bf16).T
    return (mixed, hidden_grad, jnp.concatenate(grad))


def solution(mesh):
    fine = Mesh(mesh.devices.reshape(DIMS), AXES)
    node, columns = ("y", "zl"), ("zh", "x", "c")
    return jax.shard_map(
        local,
        mesh=fine,
        in_specs=(P(node, columns), P(columns, node), P(columns, node), P(node, columns)),
        out_specs=(P(node, columns), P(node, columns), P(columns, node)),
        check_vma=False,
    )
```
